32 devices in a mesh: dp: 4 (over z), row: 2 (over core), col: 4 (over y, x).
Axes of the slice: x: 2, y: 2, z: 4, core: 2. Of those that a mesh axis runs over, the one named last changes fastest.
Arguments:
- inputs: bfloat16 [2048, 2048], P('dp', ('row', 'col')), may hold values from -11 to 11
- segments: int32 [2048], replicated, may hold values from 0 to 3, as said below
- cotangent: bfloat16 [2048, 2048], P('dp', ('row', 'col')), may hold values from -6 to 6
- w_qkv: float32 [2, 1024, 4, 640], P('row', 'dp', 'col'), may hold values from -0.1875 to 0.1875
- w_out: float32 [4, 512, 2048], P('col', 'dp', 'row'), may hold values from -0.5 to 0.5
- w_gate_up: float32 [2, 1024, 2, 5632], P('row', 'dp', None, 'col'), may hold values from -0.125 to 0.125
- w_down: float32 [4, 1408, 2048], P('col', 'dp', 'row'), may hold values from -0.078125 to 0.078125
- gains: float32 [2, 8, 256], P(None, ('row', 'col'), 'dp'), may hold values from 0.5 to 1.5
- first_qkv: float32 [2, 1024, 4, 640], P('row', 'dp', 'col'), may hold values from -29.86819 to 29.86819
- second_qkv: float32 [2, 1024, 4, 640], P('row', 'dp', 'col'), may hold values from 108.544 to 430.08
- first_out: float32 [4, 512, 2048], P('col', 'dp', 'row'), may hold values from -6.788225 to 6.788225
- second_out: float32 [4, 512, 2048], P('col', 'dp', 'row'), may hold values from 3.584 to 35.84
- first_gate_up: float32 [2, 1024, 2, 5632], P('row', 'dp', None, 'col'), may hold values from -10.589631 to 10.589631
- second_gate_up: float32 [2, 1024, 2, 5632], P('row', 'dp', None, 'col'), may hold values from 13.312 to 53.248
- first_down: float32 [4, 1408, 2048], P('col', 'dp', 'row'), may hold values from -17.920914 to 17.920914
- second_down: float32 [4, 1408, 2048], P('col', 'dp', 'row'), may hold values from 38.912 to 155.648
- first_gains: float32 [2, 8, 256], P(None, ('row', 'col'), 'dp'), may hold values from -29.86819 to 29.86819
- second_gains: float32 [2, 8, 256], P(None, ('row', 'col'), 'dp'), may hold values from 32.768 to 327.68
Outputs:
- layer_output: bfloat16 [2048, 2048], P('dp', ('row', 'col'))
- input_grad: float32 [2048, 2048], P('dp', ('row', 'col'))
- grad_qkv: float32 [2, 1024, 4, 640], P('row', 'dp', 'col')
- new_first_qkv: float32 [2, 1024, 4, 640], P('row', 'dp', 'col')
- new_second_qkv: float32 [2, 1024, 4, 640], P('row', 'dp', 'col')
- new_qkv: float32 [2, 1024, 4, 640], P('row', 'dp', 'col')
- grad_out: float32 [4, 512, 2048], P('col', 'dp', 'row')
- new_first_out: float32 [4, 512, 2048], P('col', 'dp', 'row')
- new_second_out: float32 [4, 512, 2048], P('col', 'dp', 'row')
- new_out: float32 [4, 512, 2048], P('col', 'dp', 'row')
- grad_gate_up: float32 [2, 1024, 2, 5632], P('row', 'dp', None, 'col')
- new_first_gate_up: float32 [2, 1024, 2, 5632], P('row', 'dp', None, 'col')
- new_second_gate_up: float32 [2, 1024, 2, 5632], P('row', 'dp', None, 'col')
- new_gate_up: float32 [2, 1024, 2, 5632], P('row', 'dp', None, 'col')
- grad_down: float32 [4, 1408, 2048], P('col', 'dp', 'row')
- new_first_down: float32 [4, 1408, 2048], P('col', 'dp', 'row')
- new_second_down: float32 [4, 1408, 2048], P('col', 'dp', 'row')
- new_down: float32 [4, 1408, 2048], P('col', 'dp', 'row')
- grad_gains: float32 [2, 8, 256], P(None, ('row', 'col'), 'dp')
- new_first_gains: float32 [2, 8, 256], P(None, ('row', 'col'), 'dp')
- new_second_gains: float32 [2, 8, 256], P(None, ('row', 'col'), 'dp')
- new_gains: float32 [2, 8, 256], P(None, ('row', 'col'), 'dp')
The draws below stay inside these ranges and needn't reach their ends.
Inputs may be any that keep to these rules, and one draw needn't show every extreme that they name: `segments`: segment numbers start at 0, never fall along the tokens and skip no number; each number is one document, whose tokens are consecutive and lie within one sequence of 2048 tokens; every sequence holds exactly 4 documents, one of which begins within its first 512 tokens and ends within its last 512 tokens.
All inputs are finite; a program needn't handle non-finite values.
Results may differ from the reference program's by a relative error of at most 0.017.
The reference program's roundings to bfloat16 on the way count: a program that leaves them out, or rounds other values in their place, can miss the bound.
Values may be sent and summed in bfloat16 or wider, within the bound.
A program may use at most 192 MiB of HBM per device.

```python
import math
import jax
import jax.numpy as jnp
from jax import lax

D = 2048
QH = 32
KVH = 4
HD = 64
FF = 5632
TOK_DEV = 512
STEP = 10
GQ = 8
GW = 640
TOKENS = 2048
SEQ_LEN = 2048
SEQS = 1
N_ROW = 2
N_COL = 4


def draw_inputs(key, part):
    key = jax.random.fold_in(key, 11)
    ramp = jnp.arange(D, dtype=jnp.float32) / D
    base = jnp.clip(jax.random.normal(key, (TOKENS, D), jnp.float32), -6.0, 6.0)
    scale = jnp.exp(jnp.log(0.6) + jnp.log(3.0) * ramp)
    return (base * scale[None, :]).astype(jnp.bfloat16)


def sequence_cuts(key):
    key_count, key_early, key_late = jax.random.split(key, 3)
    before = jax.random.randint(key_count, (), 0, 4).astype(jnp.int32)
    early = jnp.sort(jax.random.permutation(key_early, TOK_DEV - 1)[:3] + 1).astype(jnp.int32)
    late = jnp.sort(jax.random.permutation(key_late, TOK_DEV - 1)[:3] + (SEQ_LEN - TOK_DEV + 1)).astype(jnp.int32)
    place = jnp.arange(3, dtype=jnp.int32)
    pick = jnp.clip(place - before, 0, 2)
    return jnp.where(place < before, early, late[pick]).astype(jnp.int32)


def draw_segments(key, part):
    key = jax.random.fold_in(key, 23)
    cuts = jax.vmap(sequence_cuts)(jax.random.split(key, SEQS))
    place = jnp.arange(SEQ_LEN, dtype=jnp.int32)
    within = jnp.sum((place[None, None, :] >= cuts[:, :, None]).astype(jnp.int32), axis=1)
    offset = 4 * jnp.arange(SEQS, dtype=jnp.int32)
    return (within + offset[:, None]).reshape(TOKENS).astype(jnp.int32)


def shard_levels(key, dims, shards, low, top_value):
    level = 1.0
    for position, shards_of in shards:
        draws = jax.random.uniform(jax.random.fold_in(jax.random.fold_in(key, 6), position), (shards_of,), jnp.float32, low / len(shards), top_value / len(shards))
        level = level * jnp.repeat(jnp.exp(draws), dims[position] // shards_of).reshape((-1,) + (1,) * (len(dims) - 1 - position))
    return level


def bell_draw(rng, dims, width, reach, shards=(), kind=jnp.bfloat16):
    drawn = width * jax.random.normal(rng, dims, jnp.float32)
    if shards:
        drawn = drawn * shard_levels(rng, dims, shards, -0.22, 0.18)
    return jnp.clip(drawn, -reach, reach).astype(kind)


def setup_inputs(seed: int = 0) -> dict:
    key_of = jax.random.split(jax.random.key(seed), 19)
    inputs = draw_inputs(jax.random.fold_in(key_of[18], 71), 0)
    segments = draw_segments(jax.random.fold_in(key_of[18], 71), 0)
    cotangent = bell_draw(key_of[2], (TOKENS, D), 1.0, 6.0, ((0, 4), (1, 8)))
    w_qkv = bell_draw(key_of[3], (N_ROW, D // N_ROW, KVH, GW), (D // 2) ** -0.5, 0.1875, ((0, 2), (1, 4), (2, 4)), jnp.float32)
    w_out = bell_draw(key_of[4], (KVH, GQ * HD, D), (QH * HD // 16) ** -0.5, 0.5, ((0, 4), (1, 4), (2, 2)), jnp.float32)
    w_gate_up = bell_draw(key_of[5], (N_ROW, D // N_ROW, 2, FF), D ** -0.5, 0.125, ((0, 2), (1, 4), (3, 4)), jnp.float32)
    w_down = bell_draw(key_of[6], (N_COL, FF // N_COL, D), FF ** -0.5, 0.078125, ((0, 4), (1, 4), (2, 2)), jnp.float32)
    gains = jnp.clip(1.0 + 0.1 * jax.random.normal(key_of[7], (2, N_ROW * N_COL, D // (N_ROW * N_COL)), jnp.float32), 0.5, 1.5)
    first_qkv = bell_draw(key_of[8], (N_ROW, D // N_ROW, KVH, GW), (0.11 * TOKENS ** 0.5), 29.86819, ((0, 2), (1, 4), (2, 4)), jnp.float32)
    second_qkv = jnp.clip(jnp.exp(math.log(430.08) - 1.3768156 * jax.random.uniform(key_of[9], (N_ROW, D // N_ROW, KVH, GW), jnp.float32) ** shard_levels(key_of[9], (N_ROW, D // N_ROW, KVH, GW), ((0, 2), (1, 4), (2, 4)), -0.2, 0.2)), 108.544, 430.08)
    first_out = bell_draw(key_of[10], (KVH, GQ * HD, D), (0.025 * TOKENS ** 0.5), 6.788225, ((0, 4), (1, 4), (2, 2)), jnp.float32)
    second_out = jnp.clip(jnp.exp(math.log(35.84) - 2.3025851 * jax.random.uniform(key_of[11], (KVH, GQ * HD, D), jnp.float32) ** shard_levels(key_of[11], (KVH, GQ * HD, D), ((0, 4), (1, 4), (2, 2)), -0.2, 0.2)), 3.584, 35.84)
    first_gate_up = bell_draw(key_of[12], (N_ROW, D // N_ROW, 2, FF), (0.039 * TOKENS ** 0.5), 10.589631, ((0, 2), (1, 4), (3, 4)), jnp.float32)
    second_gate_up = jnp.clip(jnp.exp(math.log(53.248) - 1.3862944 * jax.random.uniform(key_of[13], (N_ROW, D // N_ROW, 2, FF), jnp.float32) ** shard_levels(key_of[13], (N_ROW, D // N_ROW, 2, FF), ((0, 2), (1, 4), (3, 4)), -0.2, 0.2)), 13.312, 53.248)
    first_down = bell_draw(key_of[14], (N_COL, FF // N_COL, D), (0.066 * TOKENS ** 0.5), 17.920914, ((0, 4), (1, 4), (2, 2)), jnp.float32)
    second_down = jnp.clip(jnp.exp(math.log(155.648) - 1.3862944 * jax.random.uniform(key_of[15], (N_COL, FF // N_COL, D), jnp.float32) ** shard_levels(key_of[15], (N_COL, FF // N_COL, D), ((0, 4), (1, 4), (2, 2)), -0.2, 0.2)), 38.912, 155.648)
    first_gains = bell_draw(key_of[16], (2, N_ROW * N_COL, D // (N_ROW * N_COL)), (0.11 * TOKENS ** 0.5), 29.86819, ((1, 8), (2, 4)), jnp.float32)
    second_gains = jnp.clip(jnp.exp(math.log(327.68) - 2.30258502 * jax.random.uniform(key_of[17], (2, N_ROW * N_COL, D // (N_ROW * N_COL)), jnp.float32) ** shard_levels(key_of[17], (2, N_ROW * N_COL, D // (N_ROW * N_COL)), ((1, 8), (2, 4)), -0.2, 0.2)), 32.768, 327.68)
    return dict(inputs=inputs, segments=segments, cotangent=cotangent, w_qkv=w_qkv, w_out=w_out, w_gate_up=w_gate_up, w_down=w_down, gains=gains, first_qkv=first_qkv, second_qkv=second_qkv, first_out=first_out, second_out=second_out, first_gate_up=first_gate_up, second_gate_up=second_gate_up, first_down=first_down, second_down=second_down, first_gains=first_gains, second_gains=second_gains)


@jax.custom_vjp
def low(v):
    return lax.optimization_barrier(v.astype(jnp.bfloat16)).astype(jnp.float32)

@jax.custom_vjp
def low_back(v):
    return v

def low_keep(v):
    return (low(v), None)

def low_pass(kept, grad):
    return (grad,)

def back_keep(v):
    return (v, None)

def back_low(kept, grad):
    return (low(grad),)
low.defvjp(low_keep, low_pass)
low_back.defvjp(back_keep, back_low)
NORM_EPS = 1e-05
ROPE_BASE = 10000.0
BETA_ONE = 0.9
BETA_TWO = 0.95
ADAM_EPS = 1e-08
RATE = 0.1
GAIN_RATE = 1.0
DECAY = 0.1
NEGATIVE = -1e+30

def product(left, right):
    return jnp.dot(left, right, precision=lax.Precision.HIGHEST, preferred_element_type=jnp.float32)

def rope_tables():
    place = (jnp.arange(TOKENS, dtype=jnp.int32) % SEQ_LEN).astype(jnp.float32)
    freq = ROPE_BASE ** (-(jnp.arange(HD // 2, dtype=jnp.float32) * 2.0 / HD))
    angle = place[:, None] * freq[None, :]
    return (jnp.cos(angle)[:, None, :], jnp.sin(angle)[:, None, :])

def rotate(values, cosine, sine):
    half = values.shape[-1] // 2
    first, second = (values[..., :half], values[..., half:])
    return jnp.concatenate([first * cosine - second * sine, second * cosine + first * sine], axis=-1)

def rms_norm(values, gain):
    scale = lax.rsqrt(lax.optimization_barrier(jnp.mean(values * values, axis=1, keepdims=True)) + NORM_EPS)
    return values * scale * gain[None, :]

def head_attention(item):
    queries, keys, values, segment = item
    scores = low_back(product(queries, keys.T) * 0.125)
    place = jnp.arange(SEQ_LEN, dtype=jnp.int32)
    allowed = (segment[:, None] == segment[None, :]) & (place[:, None] >= place[None, :])
    masked = jnp.where(allowed, scores, NEGATIVE)
    top = lax.optimization_barrier(jnp.max(masked, axis=1, keepdims=True))
    expo = jnp.where(allowed, jnp.exp(masked - top), 0.0)
    probs = expo / lax.optimization_barrier(jnp.sum(expo, axis=1, keepdims=True))
    return product(low(probs), values)

def heads_first(values, count):
    return values.reshape(SEQS, SEQ_LEN, count, HD).transpose(0, 2, 1, 3).reshape(SEQS * count, SEQ_LEN, HD)

def adam(weight, grad, first, second, rate, decay):
    first = BETA_ONE * first + (1.0 - BETA_ONE) * grad
    second = BETA_TWO * second + (1.0 - BETA_TWO) * grad * grad
    first_hat = first / (1.0 - BETA_ONE ** STEP)
    second_hat = second / (1.0 - BETA_TWO ** STEP)
    return (first, second, weight - rate * (first_hat / (jnp.sqrt(second_hat) + ADAM_EPS) + decay * weight))

def reference(inputs, segments, cotangent, w_qkv, w_out, w_gate_up, w_down, gains, first_qkv, second_qkv, first_out, second_out, first_gate_up, second_gate_up, first_down, second_down, first_gains, second_gains):
    cosine, sine = rope_tables()
    segment_items = jnp.repeat(segments.reshape(SEQS, SEQ_LEN), QH, axis=0)

    def forward(start, master_qkv, master_out, master_gate_up, master_down, master_gains):
        gain = low(master_gains).reshape(2, D)
        weight_qkv = low(master_qkv).reshape(D, KVH * GW)
        weight_out = low(master_out).reshape(QH * HD, D)
        weight_gate_up = low(master_gate_up).reshape(D, 2 * FF)
        weight_down = low(master_down).reshape(FF, D)
        normed = low(rms_norm(start, gain[0]))
        mixed = low_back(product(normed, weight_qkv)).reshape(TOKENS, KVH, GW)
        queries = mixed[:, :, :GQ * HD].reshape(TOKENS, QH, HD)
        keys = mixed[:, :, GQ * HD:GQ * HD + HD]
        values = mixed[:, :, GQ * HD + HD:]
        queries = low(rotate(queries, cosine, sine))
        keys = low(rotate(keys, cosine, sine))
        values = low(values)
        query_items = heads_first(queries, QH)
        key_items = heads_first(jnp.repeat(keys, GQ, axis=1), QH)
        value_items = heads_first(jnp.repeat(values, GQ, axis=1), QH)
        attended = lax.map(jax.checkpoint(head_attention), (query_items, key_items, value_items, segment_items))
        attended = attended.reshape(SEQS, QH, SEQ_LEN, HD).transpose(0, 2, 1, 3).reshape(TOKENS, QH * HD)
        attended = low_back(low(attended))
        middle = start + low_back(product(attended, weight_out))
        normed_two = low(rms_norm(middle, gain[1]))
        gate_up = low_back(product(normed_two, weight_gate_up)).reshape(TOKENS, 2, FF)
        hidden = low(jax.nn.silu(gate_up[:, 0]) * gate_up[:, 1])
        return middle + low_back(product(hidden, weight_down))
    output, pull = jax.vjp(forward, inputs.astype(jnp.float32), w_qkv, w_out, w_gate_up, w_down, gains)
    input_grad, grad_qkv, grad_out, grad_gate_up, grad_down, grad_gains = pull(cotangent.astype(jnp.float32))
    first_a, second_a, new_a = adam(w_qkv, grad_qkv, first_qkv, second_qkv, RATE, DECAY)
    first_b, second_b, new_b = adam(w_out, grad_out, first_out, second_out, RATE, DECAY)
    first_c, second_c, new_c = adam(w_gate_up, grad_gate_up, first_gate_up, second_gate_up, RATE, DECAY)
    first_d, second_d, new_d = adam(w_down, grad_down, first_down, second_down, RATE, DECAY)
    first_e, second_e, new_e = adam(gains, grad_gains, first_gains, second_gains, GAIN_RATE, 0.0)
    return (output.astype(jnp.bfloat16), input_grad, grad_qkv, first_a, second_a, new_a, grad_out, first_b, second_b, new_b, grad_gate_up, first_c, second_c, new_c, grad_down, first_d, second_d, new_d, grad_gains, first_e, second_e, new_e)
```

```python
import jax
import jax.numpy as jnp
from jax import lax
from jax.sharding import PartitionSpec as P

D = 2048
HD = 64
SEQ = 4096
STEP = 10
GQ = 8


NORM_EPS = 1e-05
ROPE_BASE = 10000.0
BETA_ONE = 0.9
BETA_TWO = 0.95
ADAM_EPS = 1e-08
RATE = 0.1
GAIN_RATE = 1.0
DECAY = 0.1
NEGATIVE = -1e30


def from_behind(array, axis, by):
    count = lax.axis_size(axis)
    pairs = [(i, i + by) for i in range(count) if 0 <= i + by < count]
    return lax.ppermute(array, axis, pairs)


def rope_tables(first, count, seq_len):
    place = ((first + jnp.arange(count, dtype=jnp.int32)) % seq_len).astype(jnp.float32)
    freq = ROPE_BASE ** (-(jnp.arange(HD // 2, dtype=jnp.float32) * 2.0 / HD))
    angle = place[:, None] * freq[None, :]
    return (jnp.cos(angle)[:, None, :], jnp.sin(angle)[:, None, :])


def rotate(values, cosine, sine):
    half = values.shape[-1] // 2
    first, second = (values[..., :half], values[..., half:])
    return jnp.concatenate(
        [first * cosine - second * sine, second * cosine + first * sine], axis=-1
    )


def unrotate(grads, cosine, sine):
    half = grads.shape[-1] // 2
    first, second = (grads[..., :half], grads[..., half:])
    return jnp.concatenate(
        [first * cosine + second * sine, second * cosine - first * sine], axis=-1
    )


def token_total(values):
    return lax.psum(values, ("row", "col"))


def width_gather(values):
    return lax.all_gather(values, "col", axis=1, tiled=True)


def column_scatter(values):
    return lax.psum_scatter(values, "col", scatter_dimension=1, tiled=True)


def row_total(values):
    return lax.psum(values, "row")


def row_gather(values):
    return lax.all_gather(values, "row", axis=1, tiled=True)


def row_scatter(values):
    return lax.psum_scatter(values, "row", scatter_dimension=1, tiled=True)


def norm_scale(values):
    return lax.rsqrt(token_total(jnp.sum(values * values, axis=1)) / D + NORM_EPS)


def norm_back(upstream, values, scale, gain):
    weighted = upstream * gain[None, :]
    total = token_total(jnp.sum(weighted * values, axis=1))
    grad = scale[:, None] * weighted - values * (scale * scale * scale * total / D)[:, None]
    gain_grad = jnp.sum(upstream * values * scale[:, None], axis=0)
    return (grad, gain_grad)


def adam(weight, grad, first, second, rate, decay):
    first = BETA_ONE * first + (1.0 - BETA_ONE) * grad
    second = BETA_TWO * second + (1.0 - BETA_TWO) * grad * grad
    first_hat = first / (1.0 - BETA_ONE**STEP)
    second_hat = second / (1.0 - BETA_TWO**STEP)
    return (
        first,
        second,
        weight - rate * (first_hat / (jnp.sqrt(second_hat) + ADAM_EPS) + decay * weight),
    )


def body(
    inputs,
    segments,
    cotangent,
    w_qkv,
    w_out,
    w_gate_up,
    w_down,
    gains,
    first_qkv,
    second_qkv,
    first_out,
    second_out,
    first_gate_up,
    second_gate_up,
    first_down,
    second_down,
    first_gains,
    second_gains,
):
    low_type = jnp.bfloat16
    count = inputs.shape[0]
    data_count = lax.axis_size("dp")
    row_count = lax.axis_size("row")
    data_place = lax.axis_index("dp")
    row_place = lax.axis_index("row")
    seq_len = min(max(SEQ, 2 * count), count * data_count)
    group = seq_len // count
    my_heads = GQ // row_count
    lowered = (
        w_qkv.astype(low_type),
        w_out.astype(low_type),
        w_gate_up.astype(low_type),
        w_down.astype(low_type),
        gains.astype(low_type),
    )
    full_qkv, full_out, full_gate_up, full_down, full_gains = (
        lax.all_gather(lowered[0], "dp", axis=1, tiled=True),
        lax.all_gather(lowered[1], "dp", axis=1, tiled=True),
        lax.all_gather(lowered[2], "dp", axis=1, tiled=True),
        lax.all_gather(lowered[3], "dp", axis=1, tiled=True),
        lax.all_gather(lowered[4], "dp", axis=2, tiled=True),
    )
    weight_qkv = full_qkv[0, :, 0, :]
    weight_out = full_out[0]
    units = full_gate_up.shape[3]
    weight_gate_up = full_gate_up[0].reshape(full_gate_up.shape[1], 2 * units)
    weight_down = full_down[0]
    gain_one = full_gains[0, 0].astype(jnp.float32)
    gain_two = full_gains[1, 0].astype(jnp.float32)
    residual = inputs.astype(jnp.float32)
    scale_one = norm_scale(residual)
    normed_one = width_gather((residual * scale_one[:, None] * gain_one[None, :]).astype(low_type))
    mixed = row_total(jnp.dot(normed_one, weight_qkv, preferred_element_type=jnp.float32))
    cosine, sine = rope_tables(data_place * count, count, seq_len)
    query_start = row_place * (my_heads * HD)
    queries = lax.dynamic_slice_in_dim(mixed, query_start, my_heads * HD, 1).reshape(
        count, my_heads, HD
    )
    queries = rotate(queries, cosine, sine).astype(low_type)
    keys = rotate(mixed[:, GQ * HD : GQ * HD + HD][:, None, :], cosine, sine)[:, 0].astype(low_type)
    values = mixed[:, GQ * HD + HD :].astype(low_type)
    query_index = data_place * count + jnp.arange(count, dtype=jnp.int32)
    query_segment = lax.dynamic_slice_in_dim(segments, data_place * count, count)
    blocks = [jnp.concatenate([keys, values], axis=1)]
    sources = [data_place]
    for step in range(1, group):
        blocks.append(from_behind(blocks[-1], "dp", 1))
        sources.append((data_place - step) % data_count)
    masks = []
    live = []
    for source in sources:
        key_index = source * count + jnp.arange(count, dtype=jnp.int32)
        key_segment = lax.dynamic_slice_in_dim(segments, source * count, count)
        masks.append(
            (query_segment[:, None] == key_segment[None, :])
            & (query_index[:, None] >= key_index[None, :])
        )
        live.append((key_segment[count - 1] >= query_segment[0]) & (source <= data_place))

    def scores_of(index):
        return (
            jnp.einsum(
                "thd,sd->hts", queries, blocks[index][:, :HD], preferred_element_type=jnp.float32
            )
            * 0.125
        )

    stats = (
        jnp.full((my_heads, count), NEGATIVE, jnp.float32),
        jnp.zeros((my_heads, count), jnp.float32),
    )
    for index in range(group):
        stats_top, stats_total = stats
        stats_masked = jnp.where(masks[index][None], scores_of(index), NEGATIVE)
        new_top = jnp.maximum(stats_top, jnp.max(stats_masked, axis=2))
        expo = jnp.where(masks[index][None], jnp.exp(stats_masked - new_top[:, :, None]), 0.0)
        stats = (new_top, stats_total * jnp.exp(stats_top - new_top) + jnp.sum(expo, axis=2))
    top, total = stats

    def probs_of(index):
        masked = jnp.where(masks[index][None], scores_of(index), NEGATIVE)
        return jnp.where(
            masks[index][None], jnp.exp(masked - top[:, :, None]) / total[:, :, None], 0.0
        )

    attended = jnp.zeros((count, my_heads, HD), jnp.float32)
    for index in range(group):
        attended = attended + jnp.einsum(
            "hts,sd->thd",
            probs_of(index).astype(low_type),
            blocks[index][:, HD:],
            preferred_element_type=jnp.float32,
        )
    heads_all = row_gather(attended.reshape(count, my_heads * HD).astype(low_type))
    middle = residual + column_scatter(
        jnp.dot(heads_all, weight_out, preferred_element_type=jnp.float32)
    )
    scale_two = norm_scale(middle)
    normed_two = width_gather((middle * scale_two[:, None] * gain_two[None, :]).astype(low_type))
    gate_up_part = jnp.dot(normed_two, weight_gate_up, preferred_element_type=jnp.float32).reshape(
        count, 2, units
    )
    gate_up = lax.psum_scatter(gate_up_part, "row", scatter_dimension=2, tiled=True)
    gate = gate_up[:, 0]
    up_value = gate_up[:, 1]
    sigma = jax.nn.sigmoid(gate)
    swish = gate * sigma
    hidden = row_gather((swish * up_value).astype(low_type))
    layer_output = (
        middle + column_scatter(jnp.dot(hidden, weight_down, preferred_element_type=jnp.float32))
    ).astype(low_type)
    down_in = width_gather(cotangent)
    grad_down = jnp.dot(hidden.T, down_in, preferred_element_type=jnp.float32)
    hidden_grad = row_scatter(jnp.dot(down_in, weight_down.T, preferred_element_type=jnp.float32))
    gate_grad = hidden_grad * up_value * sigma * (1.0 + gate * (1.0 - sigma))
    up_grad = hidden_grad * swish
    unit_grads = lax.all_gather(
        jnp.stack([gate_grad, up_grad], axis=1).astype(low_type), "row", axis=2, tiled=True
    )
    unit_grads = unit_grads.reshape(count, 2 * units)
    grad_gate_up = jnp.dot(normed_two.T, unit_grads, preferred_element_type=jnp.float32)
    normed_two_grad = column_scatter(
        jnp.dot(unit_grads, weight_gate_up.T, preferred_element_type=jnp.float32)
    )
    middle_grad, gain_two_grad = norm_back(normed_two_grad, middle, scale_two, gain_two)
    middle_grad = cotangent.astype(jnp.float32) + middle_grad
    down_term = grad_down.reshape(1, grad_down.shape[0], grad_down.shape[1])
    gate_up_term = grad_gate_up.reshape(1, grad_gate_up.shape[0], 2, units)
    branch_in = width_gather(middle_grad.astype(low_type))
    grad_out = jnp.dot(heads_all.T, branch_in, preferred_element_type=jnp.float32)
    heads_grad = row_scatter(jnp.dot(branch_in, weight_out.T, preferred_element_type=jnp.float32))
    heads_grad = heads_grad.astype(low_type).reshape(count, my_heads, HD)
    delta = jnp.sum(heads_grad.astype(jnp.float32) * attended, axis=2).T
    query_grad = jnp.zeros((count, my_heads, HD), jnp.float32)
    empty_part = jnp.zeros((count, 2 * HD), jnp.float32)
    pair_grad = empty_part
    for index in range(group):
        grad_query_grad = query_grad
        block = blocks[index]
        probs = probs_of(index)
        inner = jnp.einsum(
            "thd,sd->hts", heads_grad, block[:, HD:], preferred_element_type=jnp.float32
        )
        score_grad = (probs * (inner - delta[:, :, None])).astype(low_type)
        grad_query_grad = (
            grad_query_grad
            + jnp.einsum(
                "hts,sd->thd", score_grad, block[:, :HD], preferred_element_type=jnp.float32
            )
            * 0.125
        )
        grad_key_grad = (
            jnp.einsum("hts,thd->sd", score_grad, queries, preferred_element_type=jnp.float32)
            * 0.125
        )
        grad_value_grad = jnp.einsum(
            "hts,thd->sd", probs.astype(low_type), heads_grad, preferred_element_type=jnp.float32
        )
        query_grad = grad_query_grad
        part = jnp.concatenate([grad_key_grad, grad_value_grad], axis=1)
        if index == 0:
            pair_grad = part
        else:
            pair_grad = pair_grad + from_behind(part, "dp", -index)
    query_grad = unrotate(query_grad, cosine, sine).reshape(count, my_heads * HD)
    key_grad = unrotate(pair_grad[:, :HD][:, None, :], cosine, sine)[:, 0]
    value_grad = pair_grad[:, HD:]
    query_block = lax.dynamic_update_slice_in_dim(
        jnp.zeros((count, GQ * HD), jnp.float32), query_grad, query_start, 1
    )
    mixed_grad = row_total(jnp.concatenate([query_block, key_grad, value_grad], axis=1)).astype(
        low_type
    )
    grad_qkv = jnp.dot(normed_one.T, mixed_grad, preferred_element_type=jnp.float32)
    normed_one_grad = column_scatter(
        jnp.dot(mixed_grad, weight_qkv.T, preferred_element_type=jnp.float32)
    )
    input_grad, gain_one_grad = norm_back(normed_one_grad, residual, scale_one, gain_one)
    input_grad = middle_grad + input_grad
    qkv_term = grad_qkv.reshape(1, grad_qkv.shape[0], 1, grad_qkv.shape[1])
    out_term = grad_out.reshape(1, grad_out.shape[0], grad_out.shape[1])
    gain_term = jnp.stack([gain_one_grad, gain_two_grad], axis=0)[:, None, :]
    qkv_sum, out_sum, gate_up_sum, down_sum, gain_sum = (
        lax.psum_scatter(qkv_term, "dp", scatter_dimension=1, tiled=True),
        lax.psum_scatter(out_term, "dp", scatter_dimension=1, tiled=True),
        lax.psum_scatter(gate_up_term, "dp", scatter_dimension=1, tiled=True),
        lax.psum_scatter(down_term, "dp", scatter_dimension=1, tiled=True),
        lax.psum_scatter(gain_term, "dp", scatter_dimension=2, tiled=True),
    )
    first_a, second_a, new_a = adam(w_qkv, qkv_sum, first_qkv, second_qkv, RATE, DECAY)
    first_b, second_b, new_b = adam(w_out, out_sum, first_out, second_out, RATE, DECAY)
    first_c, second_c, new_c = adam(
        w_gate_up, gate_up_sum, first_gate_up, second_gate_up, RATE, DECAY
    )
    first_d, second_d, new_d = adam(w_down, down_sum, first_down, second_down, RATE, DECAY)
    first_e, second_e, new_e = adam(gains, gain_sum, first_gains, second_gains, GAIN_RATE, 0.0)
    return (
        layer_output,
        input_grad,
        qkv_sum,
        first_a,
        second_a,
        new_a,
        out_sum,
        first_b,
        second_b,
        new_b,
        gate_up_sum,
        first_c,
        second_c,
        new_c,
        down_sum,
        first_d,
        second_d,
        new_d,
        gain_sum,
        first_e,
        second_e,
        new_e,
    )


def gather_joint(block):
    places = lax.axis_size("dp"), lax.axis_size("col")
    rows, columns = block.shape
    parts = lax.all_gather(block, ("dp", "col"), axis=0, tiled=False)
    parts = parts.reshape(places + (rows, columns)).transpose(0, 2, 1, 3)
    return parts.reshape(places[0] * rows, places[1] * columns)


def gather_steps(block):
    return width_gather(lax.all_gather(block, "dp", axis=0, tiled=True))


def scatter_joint(whole):
    data, cols = lax.axis_size("dp"), lax.axis_size("col")
    rows, columns = whole.shape[0] // data, whole.shape[1] // cols
    parts = whole.reshape(data, rows, cols, columns).transpose(0, 2, 1, 3)
    parts = parts.reshape(data * cols, rows, columns)
    return lax.psum_scatter(parts, ("dp", "col"), scatter_dimension=0, tiled=False).astype(
        jnp.float32
    )


def scatter_steps(whole):
    part = column_scatter(whole)
    return lax.psum_scatter(part, "dp", scatter_dimension=0, tiled=True).astype(jnp.float32)


def swap(values):
    return lax.ppermute(values, "row", [(0, 1), (1, 0)])


def in_order(is_first, mine, theirs):
    return jnp.concatenate(
        [jnp.where(is_first, mine, theirs), jnp.where(is_first, theirs, mine)], axis=1
    )


def exchange(values):
    return lax.all_to_all(values, "dp", split_axis=0, concat_axis=0, tiled=True)


def dot(left, right):
    return jnp.dot(left, right, preferred_element_type=jnp.float32)


def dot_rows(left, right):
    return lax.dot_general(left, right, (((0,), (0,)), ((), ())), preferred_element_type=jnp.float32)


def dot_columns(left, right):
    return lax.dot_general(left, right, (((1,), (1,)), ((), ())), preferred_element_type=jnp.float32)


def attend(queries, keys, values, segments, block):
    tokens = queries.shape[0]
    index = jnp.arange(tokens, dtype=jnp.int32)
    outs, kept = [], []
    for start in range(0, tokens, block):
        stop = start + block
        mask = (segments[start:stop, None] == segments[None, :stop]) & (
            index[start:stop, None] >= index[None, :stop]
        )
        scores = dot_columns(queries[start:stop], keys[:stop]) * 0.125
        scores = jnp.where(mask, scores, NEGATIVE)
        expo = jnp.exp(scores - jnp.max(scores, axis=1, keepdims=True))
        expo = jnp.where(mask, expo, 0.0)
        probs = expo / jnp.sum(expo, axis=1, keepdims=True)
        outs.append(dot(probs.astype(jnp.bfloat16), values[:stop]))
        kept.append(probs)
    return jnp.concatenate(outs, axis=0), kept


def attend_back(queries, keys, values, kept, attended, upstream, block):
    tokens = queries.shape[0]
    low_type = jnp.bfloat16
    delta = jnp.sum(upstream.astype(jnp.float32) * attended, axis=1, keepdims=True)
    query_grads = []
    key_grads = [0.0] * (tokens // block)
    value_grads = [0.0] * (tokens // block)
    for place, start in enumerate(range(0, tokens, block)):
        stop = start + block
        probs = kept[place]
        inner = dot_columns(upstream[start:stop], values[:stop])
        score_grad = (probs * (inner - delta[start:stop])).astype(low_type)
        query_grads.append(dot(score_grad, keys[:stop]) * 0.125)
        key_part = dot_rows(score_grad, queries[start:stop]) * 0.125
        value_part = dot_rows(probs.astype(low_type), upstream[start:stop])
        for piece in range(place + 1):
            rows = slice(piece * block, (piece + 1) * block)
            key_grads[piece] = key_grads[piece] + key_part[rows]
            value_grads[piece] = value_grads[piece] + value_part[rows]
    return (
        jnp.concatenate(query_grads, axis=0),
        jnp.concatenate(key_grads, axis=0),
        jnp.concatenate(value_grads, axis=0),
    )


def body_units(
    inputs,
    segments,
    cotangent,
    w_qkv,
    w_out,
    w_gate_up,
    w_down,
    gains,
    first_qkv,
    second_qkv,
    first_out,
    second_out,
    first_gate_up,
    second_gate_up,
    first_down,
    second_down,
    first_gains,
    second_gains,
):
    low_type = jnp.bfloat16
    count, width = inputs.shape
    data_count = lax.axis_size("dp")
    col_count = lax.axis_size("col")
    data_place = lax.axis_index("dp")
    row_place = lax.axis_index("row")
    col_place = lax.axis_index("col")
    is_first = row_place == 0
    tokens = count * data_count
    half = width * col_count
    my_rows = w_qkv.shape[1]
    units = w_down.shape[1]
    own = units // 2

    whole_in = gather_joint(inputs)
    low_qkv = w_qkv[0, :, 0, :].astype(low_type)
    query_part = low_qkv[:, : GQ * HD].reshape(my_rows, data_count, 2 * HD).transpose(1, 0, 2)
    pair_part = jnp.broadcast_to(low_qkv[None, :, GQ * HD :], (data_count, my_rows, 2 * HD))
    weight_qkv = exchange(
        jnp.concatenate([query_part, pair_part], axis=2).reshape(data_count * my_rows, 4 * HD)
    )
    low_gains = lax.all_gather(gains[:, 0, :].astype(low_type), ("col", "dp"), axis=1, tiled=True)
    gain_one = low_gains[0].astype(jnp.float32)
    gain_two = low_gains[1].astype(jnp.float32)
    weight_gate_up = exchange(
        w_gate_up[0]
        .astype(low_type)
        .reshape(my_rows, 2, data_count, 2, own)
        .transpose(2, 0, 3, 1, 4)
        .reshape(data_count * my_rows, 4 * own)
    )
    whole_cot = gather_steps(cotangent)
    weight_out = w_out[0].astype(low_type)
    weight_down = w_down[0].astype(low_type)

    wide = whole_in.astype(jnp.float32)
    scale_one = lax.rsqrt(row_total(jnp.sum(wide * wide, axis=1)) / D + NORM_EPS)
    normed_one = (wide * scale_one[:, None] * gain_one[None, :]).astype(low_type)
    mixed = dot(normed_one, weight_qkv)
    mine = jnp.where(is_first, mixed[:, :HD], mixed[:, HD : 2 * HD])
    theirs = jnp.where(is_first, mixed[:, HD : 2 * HD], mixed[:, :HD])
    pair = mixed[:, 2 * HD :]
    arrived = swap(jnp.concatenate([theirs, pair], axis=1).astype(low_type)).astype(jnp.float32)
    mixed = jnp.concatenate([mine, pair], axis=1) + arrived
    cosine, sine = rope_tables(0, tokens, tokens)
    cosine, sine = cosine[:, 0], sine[:, 0]
    queries = rotate(mixed[:, :HD], cosine, sine).astype(low_type)
    keys = rotate(mixed[:, HD : 2 * HD], cosine, sine).astype(low_type)
    values = mixed[:, 2 * HD :].astype(low_type)
    attended, kept = attend(queries, keys, values, segments, count)
    low_attended = attended.astype(low_type)
    heads = in_order(is_first, low_attended, swap(low_attended))
    middle = inputs.astype(jnp.float32) + scatter_joint(dot(heads, weight_out).astype(low_type))
    whole_middle = gather_steps(middle.astype(low_type)).astype(jnp.float32)
    scale_two = lax.rsqrt(
        row_total(jnp.sum(whole_middle * whole_middle, axis=1)) / D + NORM_EPS
    )
    normed_two = (whole_middle * scale_two[:, None] * gain_two[None, :]).astype(low_type)

    mine_place = row_place * (2 * own)
    their_place = (1 - row_place) * (2 * own)
    mine_weight = lax.dynamic_slice_in_dim(weight_gate_up, mine_place, 2 * own, 1)
    their_weight = lax.dynamic_slice_in_dim(weight_gate_up, their_place, 2 * own, 1)
    arrived = swap(dot(normed_two, their_weight).astype(low_type))
    gate_up = dot(normed_two, mine_weight) + arrived.astype(jnp.float32)
    gate, up_value = gate_up[:, :own], gate_up[:, own:]
    sigma = jax.nn.sigmoid(gate)
    swish = gate * sigma
    low_hidden = (swish * up_value).astype(low_type)
    hidden = in_order(is_first, low_hidden, swap(low_hidden))
    down = scatter_joint(dot(hidden, weight_down).astype(low_type))
    layer_output = (middle + down).astype(low_type)

    mine_down = lax.dynamic_slice_in_dim(weight_down, row_place * own, own, 0)
    their_down = lax.dynamic_slice_in_dim(weight_down, (1 - row_place) * own, own, 0)
    arrived = swap(dot_columns(whole_cot, their_down).astype(low_type))
    hidden_grad = dot_columns(whole_cot, mine_down) + arrived.astype(jnp.float32)
    grad_down = dot_rows(hidden, whole_cot)
    gate_grad = hidden_grad * up_value * sigma * (1.0 + gate * (1.0 - sigma))
    up_grad = hidden_grad * swish
    unit_grads = jnp.concatenate([gate_grad, up_grad], axis=1).astype(low_type)
    unit_grads = in_order(is_first, unit_grads, swap(unit_grads))
    normed_two_grad = scatter_steps(dot_columns(unit_grads, weight_gate_up).astype(low_type))
    grad_gate_up = dot_rows(normed_two, unit_grads).astype(low_type)
    whole_grad = gather_joint(normed_two_grad.astype(low_type)).astype(jnp.float32)
    total_two = row_total(jnp.sum(whole_grad * gain_two[None, :] * whole_middle, axis=1))
    shrink_two = scale_two * scale_two * scale_two * total_two / D
    branch_in = (
        whole_cot.astype(jnp.float32)
        + scale_two[:, None] * (whole_grad * gain_two[None, :])
        - whole_middle * shrink_two[:, None]
    ).astype(low_type)
    gain_two_grad = jnp.sum(whole_grad * whole_middle * scale_two[:, None], axis=0)

    def my_tokens(stat):
        return lax.dynamic_slice_in_dim(stat, data_place * count, count)

    def my_width(gain):
        return lax.dynamic_slice_in_dim(gain, col_place * width, width)

    middle_grad = (
        cotangent.astype(jnp.float32)
        + my_tokens(scale_two)[:, None] * (normed_two_grad * my_width(gain_two)[None, :])
        - middle * my_tokens(shrink_two)[:, None]
    )
    grad_out = dot_rows(heads, branch_in)
    heads_grad = dot_columns(branch_in, weight_out)
    mine = jnp.where(is_first, heads_grad[:, :HD], heads_grad[:, HD:])
    theirs = jnp.where(is_first, heads_grad[:, HD:], heads_grad[:, :HD])
    heads_grad = (mine + swap(theirs.astype(low_type)).astype(jnp.float32)).astype(low_type)
    query_grad, key_grad, value_grad = attend_back(
        queries, keys, values, kept, attended, heads_grad, count
    )
    query_grad = unrotate(query_grad, cosine, sine).astype(low_type)
    pair_grad = jnp.concatenate([unrotate(key_grad, cosine, sine), value_grad], axis=1)
    sent = jnp.concatenate([query_grad, pair_grad.astype(low_type)], axis=1)
    arrived = swap(sent)
    mixed_grad = jnp.concatenate(
        [
            in_order(is_first, query_grad, arrived[:, :HD]),
            (pair_grad + arrived[:, HD:].astype(jnp.float32)).astype(low_type),
        ],
        axis=1,
    )
    part_one = dot_columns(mixed_grad, weight_qkv)
    normed_one_grad = scatter_steps(part_one.astype(low_type))
    grad_qkv = dot_rows(normed_one, mixed_grad).astype(low_type)
    weighted = part_one * wide
    token_part = jnp.sum(weighted * gain_one[None, :], axis=1)
    gain_part = lax.dynamic_update_slice_in_dim(
        jnp.zeros((2 * half,), jnp.float32),
        jnp.sum(weighted * scale_one[:, None], axis=0),
        row_place * half,
        0,
    )
    totals = lax.psum(jnp.concatenate([token_part, gain_part]), ("dp", "row", "col"))
    shrink_one = my_tokens(scale_one * scale_one * scale_one * totals[:tokens] / D)
    input_grad = (
        middle_grad
        + my_tokens(scale_one)[:, None] * (normed_one_grad * my_width(gain_one)[None, :])
        - inputs.astype(jnp.float32) * shrink_one[:, None]
    )
    share = width // data_count
    gain_start = col_place * width + data_place * share
    gain_sum = jnp.stack(
        [
            lax.dynamic_slice_in_dim(totals, tokens + row_place * half + gain_start, share),
            lax.dynamic_slice_in_dim(gain_two_grad, gain_start, share),
        ]
    )[:, None, :]
    gate_up_sum = (
        exchange(grad_gate_up)
        .reshape(data_count, my_rows, 2, 2, own)
        .transpose(1, 3, 0, 2, 4)
        .reshape(1, my_rows, 2, data_count * units)
        .astype(jnp.float32)
    )
    qkv_parts = exchange(grad_qkv).reshape(data_count, my_rows, 4 * HD).astype(jnp.float32)
    qkv_sum = jnp.concatenate(
        [
            qkv_parts[:, :, : 2 * HD].transpose(1, 0, 2).reshape(my_rows, GQ * HD),
            jnp.sum(qkv_parts[:, :, 2 * HD :], axis=0),
        ],
        axis=1,
    )[None, :, None, :]
    out_sum = grad_out[None]
    down_sum = grad_down[None]
    first_a, second_a, new_a = adam(w_qkv, qkv_sum, first_qkv, second_qkv, RATE, DECAY)
    first_b, second_b, new_b = adam(w_out, out_sum, first_out, second_out, RATE, DECAY)
    first_c, second_c, new_c = adam(
        w_gate_up, gate_up_sum, first_gate_up, second_gate_up, RATE, DECAY
    )
    first_d, second_d, new_d = adam(w_down, down_sum, first_down, second_down, RATE, DECAY)
    first_e, second_e, new_e = adam(gains, gain_sum, first_gains, second_gains, GAIN_RATE, 0.0)
    return (
        layer_output,
        input_grad,
        qkv_sum,
        first_a,
        second_a,
        new_a,
        out_sum,
        first_b,
        second_b,
        new_b,
        gate_up_sum,
        first_c,
        second_c,
        new_c,
        down_sum,
        first_d,
        second_d,
        new_d,
        gain_sum,
        first_e,
        second_e,
        new_e,
    )


def solution(mesh):
    placed = (
        P("dp", ("row", "col")),
        P(),
        P("dp", ("row", "col")),
        P("row", "dp", "col", None),
        P("col", "dp", "row"),
        P("row", "dp", None, "col"),
        P("col", "dp", "row"),
        P(None, ("row", "col"), "dp"),
        P("row", "dp", "col", None),
        P("row", "dp", "col", None),
        P("col", "dp", "row"),
        P("col", "dp", "row"),
        P("row", "dp", None, "col"),
        P("row", "dp", None, "col"),
        P("col", "dp", "row"),
        P("col", "dp", "row"),
        P(None, ("row", "col"), "dp"),
        P(None, ("row", "col"), "dp"),
    )
    whole_heads = mesh.shape["dp"] * mesh.shape["row"] == GQ and mesh.shape["row"] == 2
    return jax.shard_map(
        body_units if whole_heads else body,
        mesh=mesh,
        in_specs=placed,
        out_specs=(
            P("dp", ("row", "col")),
            P("dp", ("row", "col")),
            P("row", "dp", "col", None),
            P("row", "dp", "col", None),
            P("row", "dp", "col", None),
            P("row", "dp", "col", None),
            P("col", "dp", "row"),
            P("col", "dp", "row"),
            P("col", "dp", "row"),
            P("col", "dp", "row"),
            P("row", "dp", None, "col"),
            P("row", "dp", None, "col"),
            P("row", "dp", None, "col"),
            P("row", "dp", None, "col"),
            P("col", "dp", "row"),
            P("col", "dp", "row"),
            P("col", "dp", "row"),
            P("col", "dp", "row"),
            P(None, ("row", "col"), "dp"),
            P(None, ("row", "col"), "dp"),
            P(None, ("row", "col"), "dp"),
            P(None, ("row", "col"), "dp"),
        ),
        check_vma=False,
    )
```

```python
import jax
import jax.numpy as jnp
from jax import lax
from jax.sharding import PartitionSpec as P

D = 2048
HD = 64
SEQ = 4096
STEP = 10
GQ = 8


NORM_EPS = 1e-05
ROPE_BASE = 10000.0
BETA_ONE = 0.9
BETA_TWO = 0.95
ADAM_EPS = 1e-08
RATE = 0.1
GAIN_RATE = 1.0
DECAY = 0.1
NEGATIVE = -1e30


def from_behind(array, axis, by):
    count = lax.axis_size(axis)
    pairs = [(i, i + by) for i in range(count) if 0 <= i + by < count]
    return lax.ppermute(array, axis, pairs)


def rope_tables(first, count, seq_len):
    place = ((first + jnp.arange(count, dtype=jnp.int32)) % seq_len).astype(jnp.float32)
    freq = ROPE_BASE ** (-(jnp.arange(HD // 2, dtype=jnp.float32) * 2.0 / HD))
    angle = place[:, None] * freq[None, :]
    return (jnp.cos(angle)[:, None, :], jnp.sin(angle)[:, None, :])


def rotate(values, cosine, sine):
    half = values.shape[-1] // 2
    first, second = (values[..., :half], values[..., half:])
    return jnp.concatenate(
        [first * cosine - second * sine, second * cosine + first * sine], axis=-1
    )


def unrotate(grads, cosine, sine):
    half = grads.shape[-1] // 2
    first, second = (grads[..., :half], grads[..., half:])
    return jnp.concatenate(
        [first * cosine + second * sine, second * cosine - first * sine], axis=-1
    )


def token_total(values):
    return lax.psum(values, ("row", "col"))


def width_gather(values):
    return lax.all_gather(values, "col", axis=1, tiled=True)


def column_scatter(values):
    return lax.psum_scatter(values, "col", scatter_dimension=1, tiled=True)


def row_total(values):
    return lax.psum(values, "row")


def row_gather(values):
    return lax.all_gather(values, "row", axis=1, tiled=True)


def row_scatter(values):
    return lax.psum_scatter(values, "row", scatter_dimension=1, tiled=True)


def norm_scale(values):
    return lax.rsqrt(token_total(jnp.sum(values * values, axis=1)) / D + NORM_EPS)


def norm_back(upstream, values, scale, gain):
    weighted = upstream * gain[None, :]
    total = token_total(jnp.sum(weighted * values, axis=1))
    grad = scale[:, None] * weighted - values * (scale * scale * scale * total / D)[:, None]
    gain_grad = jnp.sum(upstream * values * scale[:, None], axis=0)
    return (grad, gain_grad)


def adam(weight, grad, first, second, rate, decay):
    first = BETA_ONE * first + (1.0 - BETA_ONE) * grad
    second = BETA_TWO * second + (1.0 - BETA_TWO) * grad * grad
    first_hat = first / (1.0 - BETA_ONE**STEP)
    second_hat = second / (1.0 - BETA_TWO**STEP)
    return (
        first,
        second,
        weight - rate * (first_hat / (jnp.sqrt(second_hat) + ADAM_EPS) + decay * weight),
    )


def body(
    inputs,
    segments,
    cotangent,
    w_qkv,
    w_out,
    w_gate_up,
    w_down,
    gains,
    first_qkv,
    second_qkv,
    first_out,
    second_out,
    first_gate_up,
    second_gate_up,
    first_down,
    second_down,
    first_gains,
    second_gains,
):
    low_type = jnp.bfloat16
    count = inputs.shape[0]
    data_count = lax.axis_size("dp")
    row_count = lax.axis_size("row")
    data_place = lax.axis_index("dp")
    row_place = lax.axis_index("row")
    seq_len = min(max(SEQ, 2 * count), count * data_count)
    group = seq_len // count
    my_heads = GQ // row_count
    lowered = (
        w_qkv.astype(low_type),
        w_out.astype(low_type),
        w_gate_up.astype(low_type),
        w_down.astype(low_type),
        gains.astype(low_type),
    )
    full_qkv, full_out, full_gate_up, full_down, full_gains = (
        lax.all_gather(lowered[0], "dp", axis=1, tiled=True),
        lax.all_gather(lowered[1], "dp", axis=1, tiled=True),
        lax.all_gather(lowered[2], "dp", axis=1, tiled=True),
        lax.all_gather(lowered[3], "dp", axis=1, tiled=True),
        lax.all_gather(lowered[4], "dp", axis=2, tiled=True),
    )
    weight_qkv = full_qkv[0, :, 0, :]
    weight_out = full_out[0]
    units = full_gate_up.shape[3]
    weight_gate_up = full_gate_up[0].reshape(full_gate_up.shape[1], 2 * units)
    weight_down = full_down[0]
    gain_one = full_gains[0, 0].astype(jnp.float32)
    gain_two = full_gains[1, 0].astype(jnp.float32)
    residual = inputs.astype(jnp.float32)
    scale_one = norm_scale(residual)
    normed_one = width_gather((residual * scale_one[:, None] * gain_one[None, :]).astype(low_type))
    mixed = row_total(jnp.dot(normed_one, weight_qkv, preferred_element_type=jnp.float32))
    cosine, sine = rope_tables(data_place * count, count, seq_len)
    query_start = row_place * (my_heads * HD)
    queries = lax.dynamic_slice_in_dim(mixed, query_start, my_heads * HD, 1).reshape(
        count, my_heads, HD
    )
    queries = rotate(queries, cosine, sine).astype(low_type)
    keys = rotate(mixed[:, GQ * HD : GQ * HD + HD][:, None, :], cosine, sine)[:, 0].astype(low_type)
    values = mixed[:, GQ * HD + HD :].astype(low_type)
    query_index = data_place * count + jnp.arange(count, dtype=jnp.int32)
    query_segment = lax.dynamic_slice_in_dim(segments, data_place * count, count)
    blocks = [jnp.concatenate([keys, values], axis=1)]
    sources = [data_place]
    for step in range(1, group):
        blocks.append(from_behind(blocks[-1], "dp", 1))
        sources.append((data_place - step) % data_count)
    masks = []
    live = []
    for source in sources:
        key_index = source * count + jnp.arange(count, dtype=jnp.int32)
        key_segment = lax.dynamic_slice_in_dim(segments, source * count, count)
        masks.append(
            (query_segment[:, None] == key_segment[None, :])
            & (query_index[:, None] >= key_index[None, :])
        )
        live.append((key_segment[count - 1] >= query_segment[0]) & (source <= data_place))

    def scores_of(index):
        return (
            jnp.einsum(
                "thd,sd->hts", queries, blocks[index][:, :HD], preferred_element_type=jnp.float32
            )
            * 0.125
        )

    stats = (
        jnp.full((my_heads, count), NEGATIVE, jnp.float32),
        jnp.zeros((my_heads, count), jnp.float32),
    )
    for index in range(group):
        stats_top, stats_total = stats
        stats_masked = jnp.where(masks[index][None], scores_of(index), NEGATIVE)
        new_top = jnp.maximum(stats_top, jnp.max(stats_masked, axis=2))
        expo = jnp.where(masks[index][None], jnp.exp(stats_masked - new_top[:, :, None]), 0.0)
        stats = (new_top, stats_total * jnp.exp(stats_top - new_top) + jnp.sum(expo, axis=2))
    top, total = stats

    def probs_of(index):
        masked = jnp.where(masks[index][None], scores_of(index), NEGATIVE)
        return jnp.where(
            masks[index][None], jnp.exp(masked - top[:, :, None]) / total[:, :, None], 0.0
        )

    attended = jnp.zeros((count, my_heads, HD), jnp.float32)
    for index in range(group):
        attended = attended + jnp.einsum(
            "hts,sd->thd",
            probs_of(index).astype(low_type),
            blocks[index][:, HD:],
            preferred_element_type=jnp.float32,
        )
    heads_all = row_gather(attended.reshape(count, my_heads * HD).astype(low_type))
    middle = residual + column_scatter(
        jnp.dot(heads_all, weight_out, preferred_element_type=jnp.float32)
    )
    scale_two = norm_scale(middle)
    normed_two = width_gather((middle * scale_two[:, None] * gain_two[None, :]).astype(low_type))
    gate_up_part = jnp.dot(normed_two, weight_gate_up, preferred_element_type=jnp.float32).reshape(
        count, 2, units
    )
    gate_up = lax.psum_scatter(gate_up_part, "row", scatter_dimension=2, tiled=True)
    gate = gate_up[:, 0]
    up_value = gate_up[:, 1]
    sigma = jax.nn.sigmoid(gate)
    swish = gate * sigma
    hidden = row_gather((swish * up_value).astype(low_type))
    layer_output = (
        middle + column_scatter(jnp.dot(hidden, weight_down, preferred_element_type=jnp.float32))
    ).astype(low_type)
    down_in = width_gather(cotangent)
    grad_down = jnp.dot(hidden.T, down_in, preferred_element_type=jnp.float32)
    hidden_grad = row_scatter(jnp.dot(down_in, weight_down.T, preferred_element_type=jnp.float32))
    gate_grad = hidden_grad * up_value * sigma * (1.0 + gate * (1.0 - sigma))
    up_grad = hidden_grad * swish
    unit_grads = lax.all_gather(
        jnp.stack([gate_grad, up_grad], axis=1).astype(low_type), "row", axis=2, tiled=True
    )
    unit_grads = unit_grads.reshape(count, 2 * units)
    grad_gate_up = jnp.dot(normed_two.T, unit_grads, preferred_element_type=jnp.float32)
    normed_two_grad = column_scatter(
        jnp.dot(unit_grads, weight_gate_up.T, preferred_element_type=jnp.float32)
    )
    middle_grad, gain_two_grad = norm_back(normed_two_grad, middle, scale_two, gain_two)
    middle_grad = cotangent.astype(jnp.float32) + middle_grad
    down_term = grad_down.reshape(1, grad_down.shape[0], grad_down.shape[1])
    gate_up_term = grad_gate_up.reshape(1, grad_gate_up.shape[0], 2, units)
    branch_in = width_gather(middle_grad.astype(low_type))
    grad_out = jnp.dot(heads_all.T, branch_in, preferred_element_type=jnp.float32)
    heads_grad = row_scatter(jnp.dot(branch_in, weight_out.T, preferred_element_type=jnp.float32))
    heads_grad = heads_grad.astype(low_type).reshape(count, my_heads, HD)
    delta = jnp.sum(heads_grad.astype(jnp.float32) * attended, axis=2).T
    query_grad = jnp.zeros((count, my_heads, HD), jnp.float32)
    empty_part = jnp.zeros((count, 2 * HD), jnp.float32)
    pair_grad = empty_part
    for index in range(group):
        grad_query_grad = query_grad
        block = blocks[index]
        probs = probs_of(index)
        inner = jnp.einsum(
            "thd,sd->hts", heads_grad, block[:, HD:], preferred_element_type=jnp.float32
        )
        score_grad = (probs * (inner - delta[:, :, None])).astype(low_type)
        grad_query_grad = (
            grad_query_grad
            + jnp.einsum(
                "hts,sd->thd", score_grad, block[:, :HD], preferred_element_type=jnp.float32
            )
            * 0.125
        )
        grad_key_grad = (
            jnp.einsum("hts,thd->sd", score_grad, queries, preferred_element_type=jnp.float32)
            * 0.125
        )
        grad_value_grad = jnp.einsum(
            "hts,thd->sd", probs.astype(low_type), heads_grad, preferred_element_type=jnp.float32
        )
        query_grad = grad_query_grad
        part = jnp.concatenate([grad_key_grad, grad_value_grad], axis=1)
        if index == 0:
            pair_grad = part
        else:
            pair_grad = pair_grad + from_behind(part, "dp", -index)
    query_grad = unrotate(query_grad, cosine, sine).reshape(count, my_heads * HD)
    key_grad = unrotate(pair_grad[:, :HD][:, None, :], cosine, sine)[:, 0]
    value_grad = pair_grad[:, HD:]
    query_block = lax.dynamic_update_slice_in_dim(
        jnp.zeros((count, GQ * HD), jnp.float32), query_grad, query_start, 1
    )
    mixed_grad = row_total(jnp.concatenate([query_block, key_grad, value_grad], axis=1)).astype(
        low_type
    )
    grad_qkv = jnp.dot(normed_one.T, mixed_grad, preferred_element_type=jnp.float32)
    normed_one_grad = column_scatter(
        jnp.dot(mixed_grad, weight_qkv.T, preferred_element_type=jnp.float32)
    )
    input_grad, gain_one_grad = norm_back(normed_one_grad, residual, scale_one, gain_one)
    input_grad = middle_grad + input_grad
    qkv_term = grad_qkv.reshape(1, grad_qkv.shape[0], 1, grad_qkv.shape[1])
    out_term = grad_out.reshape(1, grad_out.shape[0], grad_out.shape[1])
    gain_term = jnp.stack([gain_one_grad, gain_two_grad], axis=0)[:, None, :]
    qkv_sum, out_sum, gate_up_sum, down_sum, gain_sum = (
        lax.psum_scatter(qkv_term, "dp", scatter_dimension=1, tiled=True),
        lax.psum_scatter(out_term, "dp", scatter_dimension=1, tiled=True),
        lax.psum_scatter(gate_up_term, "dp", scatter_dimension=1, tiled=True),
        lax.psum_scatter(down_term, "dp", scatter_dimension=1, tiled=True),
        lax.psum_scatter(gain_term, "dp", scatter_dimension=2, tiled=True),
    )
    first_a, second_a, new_a = adam(w_qkv, qkv_sum, first_qkv, second_qkv, RATE, DECAY)
    first_b, second_b, new_b = adam(w_out, out_sum, first_out, second_out, RATE, DECAY)
    first_c, second_c, new_c = adam(
        w_gate_up, gate_up_sum, first_gate_up, second_gate_up, RATE, DECAY
    )
    first_d, second_d, new_d = adam(w_down, down_sum, first_down, second_down, RATE, DECAY)
    first_e, second_e, new_e = adam(gains, gain_sum, first_gains, second_gains, GAIN_RATE, 0.0)
    return (
        layer_output,
        input_grad,
        qkv_sum,
        first_a,
        second_a,
        new_a,
        out_sum,
        first_b,
        second_b,
        new_b,
        gate_up_sum,
        first_c,
        second_c,
        new_c,
        down_sum,
        first_d,
        second_d,
        new_d,
        gain_sum,
        first_e,
        second_e,
        new_e,
    )


def gather_steps(block):
    return width_gather(lax.all_gather(block, "dp", axis=0, tiled=True))


def scatter_steps(whole):
    part = column_scatter(whole)
    return lax.psum_scatter(part, "dp", scatter_dimension=0, tiled=True).astype(jnp.float32)


def swap(values):
    return lax.ppermute(values, "row", [(0, 1), (1, 0)])


def in_order(is_first, mine, theirs):
    return jnp.concatenate(
        [jnp.where(is_first, mine, theirs), jnp.where(is_first, theirs, mine)], axis=1
    )


def exchange(values):
    return lax.all_to_all(values, "dp", split_axis=0, concat_axis=0, tiled=True)


def dot(left, right):
    return jnp.dot(left, right, preferred_element_type=jnp.float32)


def dot_rows(left, right):
    return lax.dot_general(left, right, (((0,), (0,)), ((), ())), preferred_element_type=jnp.float32)


def dot_columns(left, right):
    return lax.dot_general(left, right, (((1,), (1,)), ((), ())), preferred_element_type=jnp.float32)


def attend(queries, keys, values, segments, block):
    tokens = queries.shape[0]
    index = jnp.arange(tokens, dtype=jnp.int32)
    outs, kept = [], []
    for start in range(0, tokens, block):
        stop = start + block
        mask = (segments[start:stop, None] == segments[None, :stop]) & (
            index[start:stop, None] >= index[None, :stop]
        )
        scores = dot_columns(queries[start:stop], keys[:stop]) * 0.125
        scores = jnp.where(mask, scores, NEGATIVE)
        expo = jnp.exp(scores - jnp.max(scores, axis=1, keepdims=True))
        expo = jnp.where(mask, expo, 0.0)
        probs = expo / jnp.sum(expo, axis=1, keepdims=True)
        outs.append(dot(probs.astype(jnp.bfloat16), values[:stop]))
        kept.append(probs)
    return jnp.concatenate(outs, axis=0), kept


def attend_back(queries, keys, values, kept, attended, upstream, block):
    tokens = queries.shape[0]
    low_type = jnp.bfloat16
    delta = jnp.sum(upstream.astype(jnp.float32) * attended, axis=1, keepdims=True)
    query_grads = []
    key_grads = [0.0] * (tokens // block)
    value_grads = [0.0] * (tokens // block)
    for place, start in enumerate(range(0, tokens, block)):
        stop = start + block
        probs = kept[place]
        inner = dot_columns(upstream[start:stop], values[:stop])
        score_grad = (probs * (inner - delta[start:stop])).astype(low_type)
        query_grads.append(dot(score_grad, keys[:stop]) * 0.125)
        key_part = dot_rows(score_grad, queries[start:stop]) * 0.125
        value_part = dot_rows(probs.astype(low_type), upstream[start:stop])
        for piece in range(place + 1):
            rows = slice(piece * block, (piece + 1) * block)
            key_grads[piece] = key_grads[piece] + key_part[rows]
            value_grads[piece] = value_grads[piece] + value_part[rows]
    return (
        jnp.concatenate(query_grads, axis=0),
        jnp.concatenate(key_grads, axis=0),
        jnp.concatenate(value_grads, axis=0),
    )


def body_units(
    inputs,
    segments,
    cotangent,
    w_qkv,
    w_out,
    w_gate_up,
    w_down,
    gains,
    first_qkv,
    second_qkv,
    first_out,
    second_out,
    first_gate_up,
    second_gate_up,
    first_down,
    second_down,
    first_gains,
    second_gains,
):
    low_type = jnp.bfloat16
    count, width = inputs.shape
    data_count = lax.axis_size("dp")
    col_count = lax.axis_size("col")
    data_place = lax.axis_index("dp")
    row_place = lax.axis_index("row")
    col_place = lax.axis_index("col")
    is_first = row_place == 0
    tokens = count * data_count
    half = width * col_count
    my_rows = w_qkv.shape[1]
    units = w_down.shape[1]
    own = units // 2

    whole_in = gather_steps(inputs)
    low_qkv = w_qkv[0, :, 0, :].astype(low_type)
    query_part = low_qkv[:, : GQ * HD].reshape(my_rows, data_count, 2 * HD).transpose(1, 0, 2)
    pair_part = jnp.broadcast_to(low_qkv[None, :, GQ * HD :], (data_count, my_rows, 2 * HD))
    weight_qkv = exchange(
        jnp.concatenate([query_part, pair_part], axis=2).reshape(data_count * my_rows, 4 * HD)
    )
    low_gains = lax.all_gather(gains[:, 0, :].astype(low_type), ("col", "dp"), axis=1, tiled=True)
    gain_one = low_gains[0].astype(jnp.float32)
    gain_two = low_gains[1].astype(jnp.float32)
    weight_gate_up = exchange(
        w_gate_up[0]
        .astype(low_type)
        .reshape(my_rows, 2, data_count, 2, own)
        .transpose(2, 0, 3, 1, 4)
        .reshape(data_count * my_rows, 4 * own)
    )
    late_cot, whole_in = lax.optimization_barrier((cotangent, whole_in))
    whole_cot = gather_steps(late_cot)
    weight_out = w_out[0].astype(low_type)
    weight_down = w_down[0].astype(low_type)

    wide = whole_in.astype(jnp.float32)
    scale_one = lax.rsqrt(row_total(jnp.sum(wide * wide, axis=1)) / D + NORM_EPS)
    normed_one = (wide * scale_one[:, None] * gain_one[None, :]).astype(low_type)
    mixed = dot(normed_one, weight_qkv)
    mine = jnp.where(is_first, mixed[:, :HD], mixed[:, HD : 2 * HD])
    theirs = jnp.where(is_first, mixed[:, HD : 2 * HD], mixed[:, :HD])
    pair = mixed[:, 2 * HD :]
    arrived = swap(jnp.concatenate([theirs, pair], axis=1).astype(low_type)).astype(jnp.float32)
    mixed = jnp.concatenate([mine, pair], axis=1) + arrived
    cosine, sine = rope_tables(0, tokens, tokens)
    cosine, sine = cosine[:, 0], sine[:, 0]
    queries = rotate(mixed[:, :HD], cosine, sine).astype(low_type)
    queries, weight_gate_up = lax.optimization_barrier((queries, weight_gate_up))
    keys = rotate(mixed[:, HD : 2 * HD], cosine, sine).astype(low_type)
    values = mixed[:, 2 * HD :].astype(low_type)
    attended, kept = attend(queries, keys, values, segments, count)
    low_attended, whole_cot = lax.optimization_barrier((attended.astype(low_type), whole_cot))
    heads = in_order(is_first, low_attended, swap(low_attended))
    middle = inputs.astype(jnp.float32) + scatter_steps(dot(heads, weight_out).astype(low_type))
    whole_middle = gather_steps(middle.astype(low_type)).astype(jnp.float32)
    scale_two = lax.rsqrt(
        row_total(jnp.sum(whole_middle * whole_middle, axis=1)) / D + NORM_EPS
    )
    normed_two = (whole_middle * scale_two[:, None] * gain_two[None, :]).astype(low_type)

    mine_place = row_place * (2 * own)
    their_place = (1 - row_place) * (2 * own)
    mine_weight = lax.dynamic_slice_in_dim(weight_gate_up, mine_place, 2 * own, 1)
    their_weight = lax.dynamic_slice_in_dim(weight_gate_up, their_place, 2 * own, 1)
    arrived = swap(dot(normed_two, their_weight).astype(low_type))
    gate_up = dot(normed_two, mine_weight) + arrived.astype(jnp.float32)
    gate, up_value = gate_up[:, :own], gate_up[:, own:]
    sigma = jax.nn.sigmoid(gate)
    swish = gate * sigma
    low_hidden = (swish * up_value).astype(low_type)
    hidden = in_order(is_first, low_hidden, swap(low_hidden))

    mine_down = lax.dynamic_slice_in_dim(weight_down, row_place * own, own, 0)
    their_down = lax.dynamic_slice_in_dim(weight_down, (1 - row_place) * own, own, 0)
    arrived = swap(dot_columns(whole_cot, their_down).astype(low_type))
    hidden_grad = dot_columns(whole_cot, mine_down) + arrived.astype(jnp.float32)
    grad_down = dot_rows(hidden, whole_cot)
    gate_grad = hidden_grad * up_value * sigma * (1.0 + gate * (1.0 - sigma))
    up_grad = hidden_grad * swish
    unit_grads = jnp.concatenate([gate_grad, up_grad], axis=1).astype(low_type)
    unit_grads = in_order(is_first, unit_grads, swap(unit_grads))
    normed_two_grad = scatter_steps(dot_columns(unit_grads, weight_gate_up).astype(low_type))
    grad_gate_up = exchange(dot_rows(normed_two, unit_grads).astype(low_type))
    whole_grad = gather_steps(normed_two_grad.astype(low_type))
    down_part = dot(hidden, weight_down).astype(low_type)
    down_part, whole_grad = lax.optimization_barrier((down_part, whole_grad))
    whole_grad = whole_grad.astype(jnp.float32)
    down = scatter_steps(down_part)
    layer_output = (middle + down).astype(low_type)
    total_two = row_total(jnp.sum(whole_grad * gain_two[None, :] * whole_middle, axis=1))
    shrink_two = scale_two * scale_two * scale_two * total_two / D
    branch_in = (
        whole_cot.astype(jnp.float32)
        + scale_two[:, None] * (whole_grad * gain_two[None, :])
        - whole_middle * shrink_two[:, None]
    ).astype(low_type)
    branch_in, grad_gate_up = lax.optimization_barrier((branch_in, grad_gate_up))
    gain_two_grad = jnp.sum(whole_grad * whole_middle * scale_two[:, None], axis=0)

    def my_tokens(stat):
        return lax.dynamic_slice_in_dim(stat, data_place * count, count)

    def my_width(gain):
        return lax.dynamic_slice_in_dim(gain, col_place * width, width)

    middle_grad = (
        cotangent.astype(jnp.float32)
        + my_tokens(scale_two)[:, None] * (normed_two_grad * my_width(gain_two)[None, :])
        - middle * my_tokens(shrink_two)[:, None]
    )
    grad_out = dot_rows(heads, branch_in)
    heads_grad = dot_columns(branch_in, weight_out)
    mine = jnp.where(is_first, heads_grad[:, :HD], heads_grad[:, HD:])
    theirs = jnp.where(is_first, heads_grad[:, HD:], heads_grad[:, :HD])
    heads_grad = (mine + swap(theirs.astype(low_type)).astype(jnp.float32)).astype(low_type)
    query_grad, key_grad, value_grad = attend_back(
        queries, keys, values, kept, attended, heads_grad, count
    )
    query_grad = unrotate(query_grad, cosine, sine).astype(low_type)
    pair_grad = jnp.concatenate([unrotate(key_grad, cosine, sine), value_grad], axis=1)
    sent = jnp.concatenate([query_grad, pair_grad.astype(low_type)], axis=1)
    arrived = swap(sent)
    mixed_grad = jnp.concatenate(
        [
            in_order(is_first, query_grad, arrived[:, :HD]),
            (pair_grad + arrived[:, HD:].astype(jnp.float32)).astype(low_type),
        ],
        axis=1,
    )
    mixed_grad, layer_output = lax.optimization_barrier((mixed_grad, layer_output))
    part_one = dot_columns(mixed_grad, weight_qkv)
    normed_one_grad = scatter_steps(part_one.astype(low_type))
    grad_qkv = dot_rows(normed_one, mixed_grad).astype(low_type)
    weighted = part_one * wide
    token_part = jnp.sum(weighted * gain_one[None, :], axis=1)
    gain_part = lax.dynamic_update_slice_in_dim(
        jnp.zeros((2 * half,), jnp.float32),
        jnp.sum(weighted * scale_one[:, None], axis=0),
        row_place * half,
        0,
    )
    totals = lax.psum(jnp.concatenate([token_part, gain_part]), ("dp", "row", "col"))
    shrink_one = my_tokens(scale_one * scale_one * scale_one * totals[:tokens] / D)
    input_grad = (
        middle_grad
        + my_tokens(scale_one)[:, None] * (normed_one_grad * my_width(gain_one)[None, :])
        - inputs.astype(jnp.float32) * shrink_one[:, None]
    )
    share = width // data_count
    gain_start = col_place * width + data_place * share
    gain_sum = jnp.stack(
        [
            lax.dynamic_slice_in_dim(totals, tokens + row_place * half + gain_start, share),
            lax.dynamic_slice_in_dim(gain_two_grad, gain_start, share),
        ]
    )[:, None, :]
    gate_up_sum = (
        grad_gate_up.reshape(data_count, my_rows, 2, 2, own)
        .transpose(1, 3, 0, 2, 4)
        .reshape(1, my_rows, 2, data_count * units)
        .astype(jnp.float32)
    )
    qkv_parts = exchange(grad_qkv).reshape(data_count, my_rows, 4 * HD).astype(jnp.float32)
    qkv_sum = jnp.concatenate(
        [
            qkv_parts[:, :, : 2 * HD].transpose(1, 0, 2).reshape(my_rows, GQ * HD),
            jnp.sum(qkv_parts[:, :, 2 * HD :], axis=0),
        ],
        axis=1,
    )[None, :, None, :]
    out_sum = grad_out[None]
    down_sum = grad_down[None]
    first_a, second_a, new_a = adam(w_qkv, qkv_sum, first_qkv, second_qkv, RATE, DECAY)
    first_b, second_b, new_b = adam(w_out, out_sum, first_out, second_out, RATE, DECAY)
    first_c, second_c, new_c = adam(
        w_gate_up, gate_up_sum, first_gate_up, second_gate_up, RATE, DECAY
    )
    first_d, second_d, new_d = adam(w_down, down_sum, first_down, second_down, RATE, DECAY)
    first_e, second_e, new_e = adam(gains, gain_sum, first_gains, second_gains, GAIN_RATE, 0.0)
    return (
        layer_output,
        input_grad,
        qkv_sum,
        first_a,
        second_a,
        new_a,
        out_sum,
        first_b,
        second_b,
        new_b,
        gate_up_sum,
        first_c,
        second_c,
        new_c,
        down_sum,
        first_d,
        second_d,
        new_d,
        gain_sum,
        first_e,
        second_e,
        new_e,
    )


def solution(mesh):
    placed = (
        P("dp", ("row", "col")),
        P(),
        P("dp", ("row", "col")),
        P("row", "dp", "col", None),
        P("col", "dp", "row"),
        P("row", "dp", None, "col"),
        P("col", "dp", "row"),
        P(None, ("row", "col"), "dp"),
        P("row", "dp", "col", None),
        P("row", "dp", "col", None),
        P("col", "dp", "row"),
        P("col", "dp", "row"),
        P("row", "dp", None, "col"),
        P("row", "dp", None, "col"),
        P("col", "dp", "row"),
        P("col", "dp", "row"),
        P(None, ("row", "col"), "dp"),
        P(None, ("row", "col"), "dp"),
    )
    whole_heads = mesh.shape["dp"] * mesh.shape["row"] == GQ and mesh.shape["row"] == 2
    return jax.shard_map(
        body_units if whole_heads else body,
        mesh=mesh,
        in_specs=placed,
        out_specs=(
            P("dp", ("row", "col")),
            P("dp", ("row", "col")),
            P("row", "dp", "col", None),
            P("row", "dp", "col", None),
            P("row", "dp", "col", None),
            P("row", "dp", "col", None),
            P("col", "dp", "row"),
            P("col", "dp", "row"),
            P("col", "dp", "row"),
            P("col", "dp", "row"),
            P("row", "dp", None, "col"),
            P("row", "dp", None, "col"),
            P("row", "dp", None, "col"),
            P("row", "dp", None, "col"),
            P("col", "dp", "row"),
            P("col", "dp", "row"),
            P("col", "dp", "row"),
            P("col", "dp", "row"),
            P(None, ("row", "col"), "dp"),
            P(None, ("row", "col"), "dp"),
            P(None, ("row", "col"), "dp"),
            P(None, ("row", "col"), "dp"),
        ),
        check_vma=False,
    )
```
